512 devices in a mesh: blk: 512 (over x, y, z, core).
Axes of the slice: x: 4, y: 4, z: 16, core: 2. Of those that a mesh axis runs over, the one named last changes fastest.
Arguments:
- points: float32 [786432, 128], P('blk'), may hold values from -6 to 6
- inv_scale: float32 [128], replicated, may hold values from 0.03 to 0.3
- vectors: float32 [786432, 64], P('blk'), may hold values from -6 to 6
Outputs:
- product: float32 [786432, 64], P('blk')
The draws below stay inside these ranges and needn't reach their ends.
All inputs are finite; a program needn't handle non-finite values.
Results may differ from the reference program's by a relative error of at most 0.0003.
Values sent between devices are 32-bit elements; how exact they have to be, the bound alone decides.
No kernel may reach another device: no remote copies, remote signals or barrier semaphores. Data moves between devices by JAX's collectives and lax.ppermute only.
A program may use at most 64 MiB of HBM per device.

```python
import math
import jax
import jax.numpy as jnp
from jax import lax

F = 128
R = 64
P_SIZE = 1536
STEPS = 2
NPTS = 786432
N_BLK = 512


def level_of(stream_key, shape, cuts, low, high):
    level, own = 1.0, jax.random.fold_in(stream_key, 6)
    for axis_at, blocks in cuts:
        steps = jnp.exp(jax.random.uniform(jax.random.fold_in(own, axis_at), (blocks,), jnp.float32, low / len(cuts), high / len(cuts)))
        level = level * jnp.repeat(steps, shape[axis_at] // blocks).reshape([-1 if axis == axis_at else 1 for axis in range(len(shape))])
    return level


def normal_values(rng, dims, deviation, most, shards=(), kind=jnp.bfloat16):
    gain = level_of(rng, dims, shards, -0.22, 0.18) if shards else 1.0
    array = jax.random.normal(rng, dims, jnp.float32) * deviation * gain
    return jnp.minimum(jnp.maximum(array, -most), most).astype(kind)


def setup_inputs(seed: int = 0) -> dict:
    key_of = jax.random.split(jax.random.key(seed), 4)
    return {
        "points": normal_values(key_of[0], (NPTS, F), 1.0, 6.0, ((0, 512),), jnp.float32),
        "inv_scale": jnp.clip(jnp.exp(jax.random.uniform(key_of[1], (F,), jnp.float32, math.log(0.03), math.log(0.3))), 0.03, 0.3),
        "vectors": normal_values(key_of[2], (NPTS, R), 1.0, 6.0, ((0, 512),), jnp.float32),
    }


def kernel_apply(left, left_sq, right, right_sq, vec):
    cross = jnp.dot(left, right.T, precision=lax.Precision.HIGHEST, preferred_element_type=jnp.float32)
    tile = jnp.exp(-0.5 * (left_sq[:, None] + right_sq[None, :] - 2.0 * cross))
    return jnp.dot(tile, vec, precision=lax.Precision.HIGHEST, preferred_element_type=jnp.float32)


def reference(points, inv_scale, vectors):
    scaled = (points * inv_scale[None, :]).reshape(N_BLK, P_SIZE, F)
    sq = jnp.sum(scaled * scaled, axis=2)
    blocks = vectors.reshape(N_BLK, P_SIZE, R)

    def one_block(index):
        total = jnp.zeros((P_SIZE, R), jnp.float32)
        for dist in range(-STEPS, STEPS + 1):
            other = ((index + dist) % N_BLK).astype(jnp.int32)
            total = total + kernel_apply(scaled[index], sq[index], scaled[other], sq[other], blocks[other])
        return total

    result = lax.map(one_block, jnp.arange(N_BLK, dtype=jnp.int32))
    return result.reshape(NPTS, R)
```

```python
import functools
import math

import jax
import jax.numpy as jnp
from jax import lax
from jax.experimental import pallas as pl
from jax.experimental.pallas import tpu as pltpu
from jax.sharding import PartitionSpec as P

F32, BF16 = jnp.float32, jnp.bfloat16
LANES = 128
WIDTH = 512
VMEM_LIMIT = 32 * 2**20


def dot(a, b, contract_b=0):
    dims = (((1,), (contract_b,)), ((), ()))
    return lax.dot_general(a, b, dims, preferred_element_type=F32)


def split(x):
    high = x.astype(BF16)
    return high, (x - high.astype(F32)).astype(BF16)


def split_points(packed, gain, points):
    scaled = packed[:points, :] * gain[...]
    high, low = split(scaled)
    h, l = high.astype(F32), low.astype(F32)
    half = -0.5 * jnp.sum(h * (h + 2.0 * l), axis=1, keepdims=True)
    first = half.astype(BF16).astype(F32)
    second = (half - first).astype(BF16).astype(F32)
    third = half - first - second
    return high, low, (first, second, third)


def place(parts, ones_at, parts_at, shape):
    lane = lax.broadcasted_iota(jnp.int32, shape, 1)
    out = jnp.where((lane >= ones_at) & (lane < ones_at + 3), 1.0, 0.0)
    for at, part in enumerate(parts):
        out = jnp.where(lane == parts_at + at, part, out)
    return out.astype(BF16)


def row_factor(packed, gain, points):
    high, low, parts = split_points(packed, gain, points)
    sq = place(parts, 3, 0, (points, LANES))
    return jnp.concatenate([high, low, high, sq], axis=1)


def column_factor(packed, gain, points):
    high, low, parts = split_points(packed, gain, points)
    sq = place(parts, 0, 3, (points, LANES))
    high_t = high.astype(F32).T.astype(BF16)
    low_t = low.astype(F32).T.astype(BF16)
    sq_t = sq.astype(F32).T.astype(BF16)
    return jnp.concatenate([high_t, high_t, low_t, sq_t], axis=0)


def split_vectors(packed, points, rhs):
    pieces = [
        packed[points + at * rhs : points + (at + 1) * rhs, :]
        for at in range(points // LANES)
    ]
    high, low = split(jnp.concatenate(pieces, axis=1))
    return jnp.concatenate([high, low], axis=0)


def apply_strip(tile_high, tile_low, vec, rhs):
    both = dot(vec, tile_high)
    return both[:rhs] + both[rhs:] + dot(vec[:rhs], tile_low)


def tile_strip(rows, column):
    return split(jnp.exp2(dot(rows, column)))


def self_kernel(points, rhs, own, gain, out, column):
    column[...] = column_factor(own, gain, points)
    rows = row_factor(own, gain, points)
    vec = split_vectors(own, points, rhs)
    for start in range(0, points, WIDTH):
        high, low = tile_strip(rows, column[:, start : start + WIDTH])
        out[:, start : start + WIDTH] = apply_strip(high, low, vec, rhs)


def gain_kernel(points, rhs, other, column, gain, total, out):
    rows = row_factor(other, gain, points)
    vec = split_vectors(other, points, rhs)
    for start in range(0, points, WIDTH):
        high, low = tile_strip(rows, column[:, start : start + WIDTH])
        out[:, start : start + WIDTH] = total[:, start : start + WIDTH] + apply_strip(
            high, low, vec, rhs
        )


def pair_kernel(points, rhs, other, own, column, gain, total, out, back):
    rows = row_factor(other, gain, points)
    vec = split_vectors(other, points, rhs)
    own_vec = split_vectors(own, points, rhs)
    partial = None
    for start in range(0, points, WIDTH):
        high, low = tile_strip(rows, column[:, start : start + WIDTH])
        out[:, start : start + WIDTH] = total[:, start : start + WIDTH] + apply_strip(
            high, low, vec, rhs
        )
        mine = own_vec[:, start : start + WIDTH]
        both = dot(mine, high, 1)
        added = both[:rhs] + both[rhs:] + dot(mine[:rhs], low, 1)
        partial = added if partial is None else partial + added
    back[...] = partial


def pack_kernel(points, rhs, pts, vec_t, out, sems):
    copies = [pltpu.make_async_copy(pts, out.at[pl.ds(0, points), :], sems.at[0])]
    for at in range(points // LANES):
        copies.append(
            pltpu.make_async_copy(
                vec_t.at[:, pl.ds(at * LANES, LANES)],
                out.at[pl.ds(points + at * rhs, rhs), :],
                sems.at[at + 1],
            )
        )
    for copy in copies:
        copy.start()
    for copy in copies:
        copy.wait()


def call(kernel, outs, tiles, points, rhs, features):
    flops = int(tiles * points * points * (8 * features + 6 * rhs))
    return pl.pallas_call(
        kernel,
        out_shape=outs,
        compiler_params=pltpu.CompilerParams(vmem_limit_bytes=VMEM_LIMIT),
        cost_estimate=pl.CostEstimate(
            flops=flops, bytes_accessed=4 * points * features, transcendentals=points * points
        ),
    )


def per_device(points, inv_scale, vectors):
    rows, features = points.shape
    rhs = vectors.shape[1]
    n = lax.axis_size("blk")
    ahead = [(i, (i - 2) % n if i % 2 == 0 else (i + 2) % n) for i in range(n)]
    back_home = [(d, s) for s, d in ahead]
    swap = [(i, i ^ 1) for i in range(n)]

    product_shape = jax.ShapeDtypeStruct((rhs, rows), F32)
    column_shape = jax.ShapeDtypeStruct((4 * features, rows), BF16)
    make = functools.partial(call, points=rows, rhs=rhs, features=features)
    bind = lambda kernel: functools.partial(kernel, rows, rhs)

    gain = (inv_scale * math.sqrt(math.log2(math.e)))[None, :]
    own = pl.pallas_call(
        bind(pack_kernel),
        out_shape=jax.ShapeDtypeStruct((rows + rhs * rows // LANES, LANES), F32),
        in_specs=[pl.BlockSpec(memory_space=pl.ANY)] * 2,
        out_specs=pl.BlockSpec(memory_space=pl.ANY),
        scratch_shapes=[pltpu.SemaphoreType.DMA((1 + rows // LANES,))],
    )(points, vectors.T)

    visitor = lax.ppermute(own, "blk", ahead)
    mate = lax.ppermute(own, "blk", swap)
    total, column = make(bind(self_kernel), (product_shape, column_shape), 1)(own, gain)
    total = make(bind(gain_kernel), product_shape, 1)(mate, column, gain, total)
    visitor, total = lax.optimization_barrier((visitor, total))
    second = lax.ppermute(visitor, "blk", swap)
    total, partial = make(bind(pair_kernel), (product_shape, product_shape), 1.5)(
        visitor, own, column, gain, total
    )
    returned = lax.ppermute(partial, "blk", back_home)
    total = make(bind(gain_kernel), product_shape, 1)(second, column, gain, total)
    return (total + returned).T


def solution(mesh):
    in_specs = (P("blk", None), P(), P("blk", None))
    out_specs = P("blk", None)
    return jax.shard_map(
        per_device, mesh=mesh, in_specs=in_specs, out_specs=out_specs, check_vma=False
    )
```

```python
import math

import jax
import jax.numpy as jnp
from jax import lax
from jax.experimental import pallas as pl
from jax.experimental.pallas import tpu as pltpu
from jax.sharding import PartitionSpec as P

F32, BF16 = jnp.float32, jnp.bfloat16
SUBLANES, LANES = 8, 128
WIDTH = 768
VMEM_LIMIT = 24 * 2**20
SELF_FLOPS = 10**9
VISIT_FLOPS = 10**10
ROOT_LOG2E = math.sqrt(math.log2(math.e))


def dot(a, b, contract_b=0):
    dims = (((1,), (contract_b,)), ((), ()))
    return lax.dot_general(a, b, dims, preferred_element_type=F32)


def split(x):
    high = x.astype(BF16)
    return high, (x - high.astype(F32)).astype(BF16)


def split_points(points, gain):
    scaled = points * (gain * ROOT_LOG2E)
    high, low = split(scaled)
    h, l = high.astype(F32), low.astype(F32)
    half = -0.5 * jnp.sum(h * (h + 2.0 * l), axis=1, keepdims=True)
    first = half.astype(BF16).astype(F32)
    second = (half - first).astype(BF16).astype(F32)
    third = half - first - second
    return high, low, (first, second, third)


def place(parts, ones_at, parts_at, shape):
    lane = lax.broadcasted_iota(jnp.int32, shape, 1)
    out = jnp.where((lane >= ones_at) & (lane < ones_at + 3), 1.0, 0.0)
    for at, part in enumerate(parts):
        out = jnp.where(lane == parts_at + at, part, out)
    return out.astype(BF16)


def row_factor(points, gain):
    high, low, parts = split_points(points, gain)
    sq = place(parts, 3, 0, (points.shape[0], LANES))
    return jnp.concatenate([high, low, high, sq], axis=1)


def column_factor(points, gain):
    high, low, parts = split_points(points, gain)
    sq = place(parts, 0, 3, (points.shape[0], LANES))
    return jnp.concatenate([high, high, low, sq], axis=1)


def split_vectors(vec_t):
    return jnp.concatenate(split(vec_t), axis=0)


def apply_strip(tile_high, tile_low, vec, rhs):
    both = dot(vec, tile_high)
    return both[:rhs] + both[rhs:] + dot(vec[:rhs], tile_low)


def tile_strip(rows, column):
    return split(jnp.exp2(dot(rows, column, 1)))


def strips(points):
    return [slice(at, at + WIDTH) for at in range(0, points, WIDTH)]


def unpack_vectors(packed, rhs, points):
    rows = range(points, points + rhs * points // LANES, rhs)
    return jnp.concatenate([packed[at : at + rhs, :] for at in rows], axis=1)


def unpack_gain(packed):
    end = packed.shape[0] - SUBLANES
    return packed[end : end + 1, :]


def self_kernel(pts, vec_t, gain, out, packed, vec_out):
    rhs, points = vec_t.shape
    packed[:points, :] = pts[...]
    for at in range(points // LANES):
        rows = slice(points + at * rhs, points + (at + 1) * rhs)
        packed[rows, :] = vec_t[:, at * LANES : (at + 1) * LANES]
    end = points + rhs * points // LANES
    packed[end:, :] = jnp.broadcast_to(gain[...], (SUBLANES, LANES))
    vec_out[...] = vec_t[...]
    column = column_factor(pts[...], gain[...])
    rows = row_factor(pts[...], gain[...])
    vec = split_vectors(vec_t[...])
    for at in strips(points):
        high, low = tile_strip(rows, column[at, :])
        out[:, at] = apply_strip(high, low, vec, rhs)


def from_columns(high, low, column_vec, rhs):
    both = dot(high, column_vec)
    return both[:, :rhs] + both[:, rhs:] + dot(low, column_vec[:, :rhs])


def column_vectors(vec_t):
    return jnp.concatenate(split(vec_t.T), axis=1)


def visit_kernel(other, own, back, tile_high, tile_low):
    rhs, points = back.shape
    vec = column_vectors(unpack_vectors(own, rhs, points))
    column = column_factor(own[:points, :], unpack_gain(own))
    rows = row_factor(other[...], unpack_gain(own))
    partial = None
    for at in strips(points):
        high, low = tile_strip(rows, column[at, :])
        tile_high[:, at] = high
        tile_low[:, at] = low
        added = from_columns(high, low, vec[at, :], rhs)
        partial = added if partial is None else partial + added
    back[...] = partial.T


def mate_kernel(core, mate, other, other_vec, own, total, partial, out, back, for_mate):
    rhs, points = total.shape
    first = core[0] == 0
    gain = unpack_gain(own)
    column = column_factor(mate[:points, :], gain)
    mate_vec = column_vectors(unpack_vectors(mate, rhs, points))
    rows = row_factor(jnp.where(first, other[...], own[:points, :]), gain)
    own_vec = unpack_vectors(own, rhs, points)
    row_vec = split_vectors(jnp.where(first, other_vec[...], own_vec))
    gained = None
    for at in strips(points):
        high, low = tile_strip(rows, column[at, :])
        for_mate[:, at] = apply_strip(high, low, row_vec, rhs)
        added = from_columns(high, low, mate_vec[at, :], rhs)
        gained = added if gained is None else gained + added
    gained = gained.T
    back[...] = partial[...] + jnp.where(first, gained, 0.0)
    out[...] = total[...] + jnp.where(first, 0.0, gained)


def apply_kernel(tile_high, tile_low, vec_t, total, out):
    rhs, points = total.shape
    vec = split_vectors(vec_t[...])
    for at in strips(points):
        out[:, at] = total[:, at] + apply_strip(tile_high[:, at], tile_low[:, at], vec, rhs)


def per_device(points, inv_scale, vectors):
    rows, features = points.shape
    rhs = vectors.shape[1]
    n = lax.axis_size("blk")
    ahead = [(i, (i - 2) % n if i % 2 == 0 else (i + 2) % n) for i in range(n)]
    back_home = [(d, s) for s, d in ahead]
    swap = [(i, i ^ 1) for i in range(n)]
    scalar, whole = [pl.BlockSpec(memory_space=space) for space in (pltpu.SMEM, pltpu.VMEM)]

    def call(kernel, outs, specs, *args, flops=1000, vmem=VMEM_LIMIT):
        return pl.pallas_call(
            kernel,
            out_shape=outs,
            in_specs=specs,
            compiler_params=pltpu.CompilerParams(vmem_limit_bytes=vmem),
            cost_estimate=pl.CostEstimate(
                flops=flops, bytes_accessed=rows, transcendentals=rows
            ),
        )(*args)

    core = (lax.axis_index("blk") % 2)[None]
    gain = inv_scale[None, :]
    vec_t = vectors.T
    product = jax.ShapeDtypeStruct((rhs, rows), F32)
    tile = jax.ShapeDtypeStruct((rows, rows), BF16)
    packed = jax.ShapeDtypeStruct((rows + rhs * rows // LANES + SUBLANES, LANES), F32)

    visitor = lax.ppermute(points, "blk", ahead)
    total, own, vec_copy = call(
        self_kernel, (product, packed, product), [whole] * 3, points, vec_t, gain, flops=SELF_FLOPS
    )
    mate = lax.ppermute(own, "blk", swap)
    visitor_vec = lax.ppermute(vec_copy, "blk", ahead)
    partial, high, low = call(
        visit_kernel,
        (product, tile, tile),
        [whole] * 2,
        *(visitor, own),
        flops=VISIT_FLOPS,
    )
    total, partial, for_mate = call(
        mate_kernel,
        (product, product, product),
        [scalar] + [whole] * 6,
        *(core, mate, visitor, visitor_vec, own, total, partial),
        flops=SELF_FLOPS,
    )
    returned = lax.ppermute(partial, "blk", back_home)
    from_chip = lax.ppermute(for_mate, "blk", swap)
    total = call(apply_kernel, product, [whole] * 4, high, low, visitor_vec, total)
    return (total + returned + from_chip).T


def solution(mesh):
    in_specs = (P("blk", None), P(), P("blk", None))
    out_specs = P("blk", None)
    return jax.shard_map(
        per_device, mesh=mesh, in_specs=in_specs, out_specs=out_specs, check_vma=False
    )
```

```python
import math

import jax
import jax.numpy as jnp
from jax import lax
from jax.experimental import pallas as pl
from jax.experimental.pallas import tpu as pltpu
from jax.sharding import PartitionSpec as P

F32, BF16 = jnp.float32, jnp.bfloat16
SUBLANES, LANES = 8, 128
WIDTH = 768
VMEM_LIMIT = 24 * 2**20
SELF_FLOPS = 10**9
VISIT_FLOPS = 10**10
ROOT_LOG2E = math.sqrt(math.log2(math.e))


def dot(a, b, contract_b=0):
    dims = (((1,), (contract_b,)), ((), ()))
    return lax.dot_general(a, b, dims, preferred_element_type=F32)


def split(x):
    high = x.astype(BF16)
    return high, (x - high.astype(F32)).astype(BF16)


def split_points(points, gain):
    scaled = points * (gain * ROOT_LOG2E)
    high, low = split(scaled)
    h, l = high.astype(F32), low.astype(F32)
    half = -0.5 * jnp.sum(h * (h + 2.0 * l), axis=1, keepdims=True)
    first = half.astype(BF16).astype(F32)
    second = (half - first).astype(BF16).astype(F32)
    third = half - first - second
    return high, low, (first, second, third)


def place(parts, ones_at, parts_at, points, lane):
    ones = jnp.where((lane >= ones_at) & (lane < ones_at + 3), 1.0, 0.0)
    out = jnp.broadcast_to(ones, (points, LANES))
    for at, part in enumerate(parts):
        out = jnp.where(lane == parts_at + at, part, out)
    return out.astype(BF16)


def lanes():
    return lax.broadcasted_iota(jnp.int32, (1, LANES), 1)


def row_factor(points, gain, lane=None):
    high, low, parts = split_points(points, gain)
    sq = place(parts, 3, 0, points.shape[0], lanes() if lane is None else lane)
    return jnp.concatenate([high, low, high, sq], axis=1)


def column_factor(points, gain, lane=None):
    high, low, parts = split_points(points, gain)
    sq = place(parts, 0, 3, points.shape[0], lanes() if lane is None else lane)
    return jnp.concatenate([high, high, low, sq], axis=1)


def split_vectors(vec_t):
    return jnp.concatenate(split(vec_t), axis=0)


def apply_strip(tile_high, tile_low, vec, rhs):
    both = dot(vec, tile_high)
    return both[:rhs] + both[rhs:] + dot(vec[:rhs], tile_low)


def tile_strip(rows, column):
    return split(jnp.exp2(dot(rows, column, 1)))


def strips(points):
    return [slice(at, at + WIDTH) for at in range(0, points, WIDTH)]


def unpack_vectors(packed, rhs, points):
    rows = range(points, points + rhs * points // LANES, rhs)
    return jnp.concatenate([packed[at : at + rhs, :] for at in rows], axis=1)


def unpack_gain(packed):
    end = packed.shape[0] - SUBLANES
    return packed[end : end + 1, :]


def lane_kernel(out):
    out[...] = lax.broadcasted_iota(jnp.int32, out.shape, 1)


def self_kernel(lane, pts, vec_t, gain, out, packed, vec_out):
    rhs, points = vec_t.shape
    packed[:points, :] = pts[...]
    for at in range(points // LANES):
        rows = slice(points + at * rhs, points + (at + 1) * rhs)
        packed[rows, :] = vec_t[:, at * LANES : (at + 1) * LANES]
    end = points + rhs * points // LANES
    packed[end:, :] = jnp.broadcast_to(gain[...], (SUBLANES, LANES))
    vec_out[...] = vec_t[...]
    column = column_factor(pts[...], gain[...], lane[:1, :])
    rows = row_factor(pts[...], gain[...], lane[:1, :])
    vec = split_vectors(vec_t[...])
    for at in strips(points):
        high, low = tile_strip(rows, column[at, :])
        out[:, at] = apply_strip(high, low, vec, rhs)


def from_columns(high, low, column_vec, rhs):
    both = dot(high, column_vec)
    return both[:, :rhs] + both[:, rhs:] + dot(low, column_vec[:, :rhs])


def column_vectors(vec_t):
    return jnp.concatenate(split(vec_t.T), axis=1)


def visit_kernel(other, own, back, tile_high, tile_low):
    rhs, points = back.shape
    gain = unpack_gain(own)
    vec = column_vectors(unpack_vectors(own, rhs, points))
    column = column_factor(own[:points, :], gain)
    rows = row_factor(other[...], gain)
    partial = None
    for at in strips(points):
        high, low = tile_strip(rows, column[at, :])
        tile_high[:, at] = high
        tile_low[:, at] = low
        added = from_columns(high, low, vec[at, :], rhs)
        partial = added if partial is None else partial + added
    back[...] = partial.T


def mate_kernel(other, mate, partial, back):
    rhs, points = back.shape
    gain = unpack_gain(mate)
    rows = row_factor(mate[:points, :], gain)
    vec = split_vectors(unpack_vectors(mate, rhs, points))
    column = column_factor(other[...], gain)
    for at in strips(points):
        high, low = tile_strip(rows, column[at, :])
        back[:, at] = partial[:, at] + apply_strip(high, low, vec, rhs)


def own_kernel(tile_high, tile_low, other_vec, own, mate, out):
    rhs, points = out.shape
    gain = unpack_gain(own)
    vec = split_vectors(other_vec[...])
    column = column_factor(own[:points, :], gain)
    rows = row_factor(mate[:points, :], gain)
    mate_vec = split_vectors(unpack_vectors(mate, rhs, points))
    for at in strips(points):
        gained = apply_strip(tile_high[:, at], tile_low[:, at], vec, rhs)
        high, low = tile_strip(rows, column[at, :])
        out[:, at] = gained + apply_strip(high, low, mate_vec, rhs)


def per_device(points, inv_scale, vectors):
    rows, features = points.shape
    rhs = vectors.shape[1]
    n = lax.axis_size("blk")
    ahead = [(i, (i - 2) % n if i % 2 == 0 else (i + 2) % n) for i in range(n)]
    back_home = [(d, s) for s, d in ahead]
    swap = [(i, i ^ 1) for i in range(n)]
    def call(kernel, outs, *args, flops):
        return pl.pallas_call(
            kernel,
            out_shape=outs,
            compiler_params=pltpu.CompilerParams(vmem_limit_bytes=VMEM_LIMIT),
            cost_estimate=pl.CostEstimate(
                flops=flops, bytes_accessed=rows, transcendentals=rows
            ),
        )(*args)

    gain = inv_scale[None, :]
    vec_t = vectors.T
    product = jax.ShapeDtypeStruct((rhs, rows), F32)
    tile = jax.ShapeDtypeStruct((rows, rows), BF16)
    packed = jax.ShapeDtypeStruct((rows + rhs * rows // LANES + SUBLANES, LANES), F32)

    visitor = lax.ppermute(points, "blk", ahead)
    lane_shape = jax.ShapeDtypeStruct((SUBLANES, LANES), jnp.int32)
    lane = call(lane_kernel, lane_shape, flops=VISIT_FLOPS)
    total, own, vec_copy = call(
        self_kernel,
        (product, packed, product),
        *(lane, points, vec_t, gain),
        flops=SELF_FLOPS,
    )
    mate = lax.ppermute(own, "blk", swap)
    visitor_vec = lax.ppermute(vec_copy, "blk", ahead)
    partial, high, low = call(
        visit_kernel, (product, tile, tile), visitor, own, flops=VISIT_FLOPS
    )
    partial = call(mate_kernel, product, visitor, mate, partial, flops=SELF_FLOPS)
    returned = lax.ppermute(partial, "blk", back_home)
    gained = call(own_kernel, product, high, low, visitor_vec, own, mate, flops=SELF_FLOPS)
    return (total + gained + returned).T


def solution(mesh):
    in_specs = (P("blk", None), P(), P("blk", None))
    out_specs = P("blk", None)
    return jax.shard_map(
        per_device, mesh=mesh, in_specs=in_specs, out_specs=out_specs, check_vma=False
    )
```

```python
import math

import jax
import jax.numpy as jnp
from jax import lax
from jax.experimental import pallas as pl
from jax.experimental.pallas import tpu as pltpu
from jax.sharding import PartitionSpec as P

F32, BF16, F8 = jnp.float32, jnp.bfloat16, jnp.float8_e4m3fn
TILE_SCALE, VEC_SCALE = 2.0**16, 256.0
SUBLANES, LANES = 8, 128
WIDTH = 768
VMEM_LIMIT = 24 * 2**20
MOST_FLOPS = 10**10
LANE_FLOPS = 10**10
SELF_FLOPS = 10**9
VISIT_FLOPS = 3 * 10**9
ROOT_LOG2E = math.sqrt(math.log2(math.e))


def dot(a, b, contract_b=0):
    dims = (((1,), (contract_b,)), ((), ()))
    return lax.dot_general(a, b, dims, preferred_element_type=F32)


def split(x):
    high = x.astype(BF16)
    return high, (x - high.astype(F32)).astype(BF16)


def split_points(points, gain):
    scaled = points * (gain * ROOT_LOG2E)
    high, low = split(scaled)
    h, l = high.astype(F32), low.astype(F32)
    half = -0.5 * jnp.sum(h * (h + 2.0 * l), axis=1, keepdims=True)
    first = half.astype(BF16).astype(F32)
    second = (half - first).astype(BF16).astype(F32)
    third = half - first - second
    return high, low, (first, second, third)


def place(parts, ones_at, parts_at, points, lane):
    ones = jnp.where((lane >= ones_at) & (lane < ones_at + 3), 1.0, 0.0)
    out = jnp.broadcast_to(ones, (points, LANES))
    for at, part in enumerate(parts):
        out = jnp.where(lane == parts_at + at, part, out)
    return out.astype(BF16)


def lanes():
    return lax.broadcasted_iota(jnp.int32, (1, LANES), 1)


def row_factor(points, gain, lane=None):
    high, low, parts = split_points(points, gain)
    sq = place(parts, 3, 0, points.shape[0], lanes() if lane is None else lane)
    return jnp.concatenate([high, low, high, sq], axis=1)


def column_factor(points, gain, lane=None):
    high, low, parts = split_points(points, gain)
    sq = place(parts, 0, 3, points.shape[0], lanes() if lane is None else lane)
    return jnp.concatenate([high, high, low, sq], axis=1)


def vector_parts(vec, axis, most=None):
    if most is None:
        most = jnp.max(jnp.abs(vec))
    most = jnp.maximum(most, 1e-30)
    coarse = (vec * (VEC_SCALE / most)).astype(F8)
    return jnp.concatenate(split(vec), axis=axis), coarse, most / (VEC_SCALE * TILE_SCALE)


def split_vectors(vec_t, most=None):
    return vector_parts(vec_t, 0, most)


def column_vectors(vec_t):
    return vector_parts(vec_t.T, 1)


def apply_strip(tile_high, tile_low, vec, rhs):
    both = dot(vec[0], tile_high)
    return both[:rhs] + both[rhs:] + dot(vec[1], tile_low) * vec[2]


def tile_strip(rows, column):
    tile = jnp.exp2(dot(rows, column, 1))
    high = tile.astype(BF16)
    return high, ((tile - high.astype(F32)) * TILE_SCALE).astype(F8)


def strips(points):
    return [slice(at, at + WIDTH) for at in range(0, points, WIDTH)]


def unpack_vectors(packed, rhs, points):
    rows = range(points, points + rhs * points // LANES, rhs)
    return jnp.concatenate([packed[at : at + rhs, :] for at in rows], axis=1)


def unpack_gain(packed):
    end = packed.shape[0] - SUBLANES
    return packed[end : end + 1, :]


def lane_kernel(out):
    out[...] = lax.broadcasted_iota(jnp.int32, out.shape, 1)


def self_kernel(lane, pts, vec_t, gain, out, packed, vec_out):
    rhs, points = vec_t.shape
    packed[:points, :] = pts[...]
    for at in range(points // LANES):
        rows = slice(points + at * rhs, points + (at + 1) * rhs)
        packed[rows, :] = vec_t[:, at * LANES : (at + 1) * LANES]
    end = points + rhs * points // LANES
    packed[end:, :] = jnp.broadcast_to(gain[...], (SUBLANES, LANES))
    vec_out[...] = vec_t[...]
    column = column_factor(pts[...], gain[...], lane[:1, :])
    rows = row_factor(pts[...], gain[...], lane[:1, :])
    vec = split_vectors(vec_t[...])
    for at in strips(points):
        high, low = tile_strip(rows, column[at, :])
        out[:, at] = apply_strip(high, low, vec, rhs)


def from_columns(high, low, vec, at, rhs):
    both = dot(high, vec[0][at, :])
    return both[:, :rhs] + both[:, rhs:] + dot(low, vec[1][at, :]) * vec[2]


def visit_kernel(other, own, back, tile_high, tile_low):
    rhs, points = back.shape
    gain = unpack_gain(own)
    vec = column_vectors(unpack_vectors(own, rhs, points))
    column = column_factor(own[:points, :], gain)
    rows = row_factor(other[...], gain)
    partial = None
    for at in strips(points):
        high, low = tile_strip(rows, column[at, :])
        tile_high[:, at] = high
        tile_low[:, at] = low
        added = from_columns(high, low, vec, at, rhs)
        partial = added if partial is None else partial + added
    back[...] = partial.T


def most_kernel(vec_t, after, out):
    out[...] = jnp.full(out.shape, jnp.max(jnp.abs(vec_t[...])), F32)


def mate_kernel(other, mate, partial, most, back, most_out):
    rhs, points = back.shape
    most_out[...] = most[...]
    gain = unpack_gain(mate)
    rows = row_factor(mate[:points, :], gain)
    vec = split_vectors(unpack_vectors(mate, rhs, points))
    column = column_factor(other[...], gain)
    for at in strips(points):
        high, low = tile_strip(rows, column[at, :])
        back[:, at] = partial[:, at] + apply_strip(high, low, vec, rhs)


def own_kernel(tile_high, tile_low, other_vec, most, own, mate, out):
    rhs, points = out.shape
    gain = unpack_gain(own)
    vec = split_vectors(other_vec[...], most[:1, :1])
    column = column_factor(own[:points, :], gain)
    rows = row_factor(mate[:points, :], gain)
    mate_vec = split_vectors(unpack_vectors(mate, rhs, points))
    for at in strips(points):
        gained = apply_strip(tile_high[:, at], tile_low[:, at], vec, rhs)
        high, low = tile_strip(rows, column[at, :])
        out[:, at] = gained + apply_strip(high, low, mate_vec, rhs)


def per_device(points, inv_scale, vectors):
    rows, features = points.shape
    rhs = vectors.shape[1]
    n = lax.axis_size("blk")
    ahead = [(i, (i - 2) % n if i % 2 == 0 else (i + 2) % n) for i in range(n)]
    back_home = [(d, s) for s, d in ahead]
    swap = [(i, i ^ 1) for i in range(n)]
    def call(kernel, outs, *args, flops):
        return pl.pallas_call(
            kernel,
            out_shape=outs,
            compiler_params=pltpu.CompilerParams(vmem_limit_bytes=VMEM_LIMIT),
            cost_estimate=pl.CostEstimate(
                flops=flops, bytes_accessed=rows, transcendentals=rows
            ),
        )(*args)

    gain = inv_scale[None, :]
    vec_t = vectors.T
    product = jax.ShapeDtypeStruct((rhs, rows), F32)
    tile, rest = [jax.ShapeDtypeStruct((rows, rows), kind) for kind in (BF16, F8)]
    packed = jax.ShapeDtypeStruct((rows + rhs * rows // LANES + SUBLANES, LANES), F32)

    visitor = lax.ppermute(points, "blk", ahead)
    lane_shape = jax.ShapeDtypeStruct((SUBLANES, LANES), jnp.int32)
    lane = call(lane_kernel, lane_shape, flops=LANE_FLOPS)
    total, own, vec_copy = call(
        self_kernel,
        (product, packed, product),
        *(lane, points, vec_t, gain),
        flops=SELF_FLOPS,
    )
    mate = lax.ppermute(own, "blk", swap)
    visitor_vec = lax.ppermute(vec_copy, "blk", ahead)
    partial, high, low = call(
        visit_kernel, (product, tile, rest), visitor, own, flops=VISIT_FLOPS
    )
    most_shape = jax.ShapeDtypeStruct((SUBLANES, LANES), F32)
    most = call(most_kernel, most_shape, visitor_vec, partial, flops=MOST_FLOPS)
    partial, most = call(
        mate_kernel, (product, most_shape), visitor, mate, partial, most, flops=SELF_FLOPS
    )
    returned = lax.ppermute(partial, "blk", back_home)
    gained = call(
        own_kernel, product, *(high, low, visitor_vec, most, own, mate), flops=SELF_FLOPS
    )
    return (total + gained + returned).T


def solution(mesh):
    in_specs = (P("blk", None), P(), P("blk", None))
    out_specs = P("blk", None)
    return jax.shard_map(
        per_device, mesh=mesh, in_specs=in_specs, out_specs=out_specs, check_vma=False
    )
```

```python
import math

import jax
import jax.numpy as jnp
from jax import lax
from jax.experimental import pallas as pl
from jax.experimental.pallas import tpu as pltpu
from jax.sharding import PartitionSpec as P

F32, BF16, F8 = jnp.float32, jnp.bfloat16, jnp.float8_e4m3fn
TILE_SCALE, VEC_SCALE = 2.0**16, 256.0
SUBLANES, LANES = 8, 128
WIDTH = 1536
VMEM_LIMIT = 36 * 2**20
MOST_FLOPS = 10**10
LANE_FLOPS = 10**10
SELF_FLOPS = 10**9
VISIT_FLOPS = 3 * 10**9
ROOT_LOG2E = math.sqrt(math.log2(math.e))


def dot(a, b, contract_b=0):
    dims = (((1,), (contract_b,)), ((), ()))
    return lax.dot_general(a, b, dims, preferred_element_type=F32)


def split(x):
    high = x.astype(BF16)
    return high, (x - high.astype(F32)).astype(BF16)


def split_points(points, gain):
    scaled = points * (gain * ROOT_LOG2E)
    high, low = split(scaled)
    h, l = high.astype(F32), low.astype(F32)
    half = -0.5 * jnp.sum(h * (h + 2.0 * l), axis=1, keepdims=True)
    first = half.astype(BF16).astype(F32)
    second = (half - first).astype(BF16).astype(F32)
    third = half - first - second
    return high, low, (first, second, third)


def place(parts, ones_at, parts_at, points, lane):
    ones = jnp.where((lane >= ones_at) & (lane < ones_at + 3), 1.0, 0.0)
    out = jnp.broadcast_to(ones, (points, LANES))
    for at, part in enumerate(parts):
        out = jnp.where(lane == parts_at + at, part, out)
    return out.astype(BF16)


def lanes():
    return lax.broadcasted_iota(jnp.int32, (1, LANES), 1)


def row_factor(points, gain, lane=None):
    high, low, parts = split_points(points, gain)
    sq = place(parts, 3, 0, points.shape[0], lanes() if lane is None else lane)
    return jnp.concatenate([high, low, high, sq], axis=1)


def column_factor(points, gain, lane=None):
    high, low, parts = split_points(points, gain)
    sq = place(parts, 0, 3, points.shape[0], lanes() if lane is None else lane)
    return jnp.concatenate([high, high, low, sq], axis=1)


def vector_parts(vec, axis, most=None):
    if most is None:
        most = jnp.max(jnp.abs(vec))
    most = jnp.maximum(most, 1e-30)
    coarse = (vec * (VEC_SCALE / most)).astype(F8)
    return jnp.concatenate(split(vec), axis=axis), coarse, most / (VEC_SCALE * TILE_SCALE)


def split_vectors(vec_t, most=None):
    return vector_parts(vec_t, 0, most)


def column_vectors(vec_t):
    return vector_parts(vec_t.T, 1)


def apply_strip(tile_high, tile_low, vec, rhs):
    both = dot(vec[0], tile_high)
    return both[:rhs] + both[rhs:] + dot(vec[1], tile_low) * vec[2]


def tile_strip(rows, column):
    tile = jnp.exp2(dot(rows, column, 1))
    high = tile.astype(BF16)
    return high, ((tile - high.astype(F32)) * TILE_SCALE).astype(F8)


def strips(points):
    return [slice(at, at + WIDTH) for at in range(0, points, WIDTH)]


def unpack_vectors(packed, rhs, points):
    rows = range(points, points + rhs * points // LANES, rhs)
    return jnp.concatenate([packed[at : at + rhs, :] for at in rows], axis=1)


def unpack_gain(packed):
    end = packed.shape[0] - SUBLANES
    return packed[end : end + 1, :]


def lane_kernel(out):
    out[...] = lax.broadcasted_iota(jnp.int32, out.shape, 1)


def self_kernel(lane, pts, vec_t, gain, out, packed, vec_out):
    rhs, points = vec_t.shape
    packed[:points, :] = pts[...]
    for at in range(points // LANES):
        rows = slice(points + at * rhs, points + (at + 1) * rhs)
        packed[rows, :] = vec_t[:, at * LANES : (at + 1) * LANES]
    end = points + rhs * points // LANES
    packed[end:, :] = jnp.broadcast_to(gain[...], (SUBLANES, LANES))
    vec_out[...] = vec_t[...]
    column = column_factor(pts[...], gain[...], lane[:1, :])
    rows = row_factor(pts[...], gain[...], lane[:1, :])
    vec = split_vectors(vec_t[...])
    for at in strips(points):
        high, low = tile_strip(rows, column[at, :])
        out[:, at] = apply_strip(high, low, vec, rhs)


def from_columns(high, low, vec, at, rhs):
    both = dot(high, vec[0][at, :])
    return both[:, :rhs] + both[:, rhs:] + dot(low, vec[1][at, :]) * vec[2]


def visit_kernel(other, own, back, tile_high, tile_low):
    rhs, points = back.shape
    gain = unpack_gain(own)
    vec = column_vectors(unpack_vectors(own, rhs, points))
    column = column_factor(own[:points, :], gain)
    rows = row_factor(other[...], gain)
    partial = None
    for at in strips(points):
        high, low = tile_strip(rows, column[at, :])
        tile_high[:, at] = high
        tile_low[:, at] = low
        added = from_columns(high, low, vec, at, rhs)
        partial = added if partial is None else partial + added
    back[...] = partial.T


def most_kernel(vec_t, after, out):
    out[...] = jnp.full(out.shape, jnp.max(jnp.abs(vec_t[...])), F32)


def mate_kernel(other, mate, partial, most, back, most_out):
    rhs, points = back.shape
    most_out[...] = most[...]
    gain = unpack_gain(mate)
    rows = row_factor(mate[:points, :], gain)
    vec = split_vectors(unpack_vectors(mate, rhs, points))
    column = column_factor(other[...], gain)
    for at in strips(points):
        high, low = tile_strip(rows, column[at, :])
        back[:, at] = partial[:, at] + apply_strip(high, low, vec, rhs)


def own_kernel(tile_high, tile_low, other_vec, most, own, mate, out):
    rhs, points = out.shape
    gain = unpack_gain(own)
    vec = split_vectors(other_vec[...], most[:1, :1])
    column = column_factor(own[:points, :], gain)
    rows = row_factor(mate[:points, :], gain)
    mate_vec = split_vectors(unpack_vectors(mate, rhs, points))
    for at in strips(points):
        gained = apply_strip(tile_high[:, at], tile_low[:, at], vec, rhs)
        high, low = tile_strip(rows, column[at, :])
        out[:, at] = gained + apply_strip(high, low, mate_vec, rhs)


def per_device(points, inv_scale, vectors):
    rows, features = points.shape
    rhs = vectors.shape[1]
    n = lax.axis_size("blk")
    ahead = [(i, (i - 2) % n if i % 2 == 0 else (i + 2) % n) for i in range(n)]
    back_home = [(d, s) for s, d in ahead]
    swap = [(i, i ^ 1) for i in range(n)]
    def call(kernel, outs, *args, flops):
        return pl.pallas_call(
            kernel,
            out_shape=outs,
            compiler_params=pltpu.CompilerParams(vmem_limit_bytes=VMEM_LIMIT),
            cost_estimate=pl.CostEstimate(
                flops=flops, bytes_accessed=rows, transcendentals=rows
            ),
        )(*args)

    gain = inv_scale[None, :]
    vec_t = vectors.T
    product = jax.ShapeDtypeStruct((rhs, rows), F32)
    tile, rest = [jax.ShapeDtypeStruct((rows, rows), kind) for kind in (BF16, F8)]
    packed = jax.ShapeDtypeStruct((rows + rhs * rows // LANES + SUBLANES, LANES), F32)

    visitor = lax.ppermute(points, "blk", ahead)
    lane_shape = jax.ShapeDtypeStruct((SUBLANES, LANES), jnp.int32)
    lane = call(lane_kernel, lane_shape, flops=LANE_FLOPS)
    total, own, vec_copy = call(
        self_kernel,
        (product, packed, product),
        *(lane, points, vec_t, gain),
        flops=SELF_FLOPS,
    )
    mate = lax.ppermute(own, "blk", swap)
    visitor_vec = lax.ppermute(vec_copy, "blk", ahead)
    partial, high, low = call(
        visit_kernel, (product, tile, rest), visitor, own, flops=VISIT_FLOPS
    )
    most_shape = jax.ShapeDtypeStruct((SUBLANES, LANES), F32)
    most = call(most_kernel, most_shape, visitor_vec, partial, flops=MOST_FLOPS)
    partial, most = call(
        mate_kernel, (product, most_shape), visitor, mate, partial, most, flops=SELF_FLOPS
    )
    returned = lax.ppermute(partial, "blk", back_home)
    gained = call(
        own_kernel, product, *(high, low, visitor_vec, most, own, mate), flops=SELF_FLOPS
    )
    return (total + gained + returned).T


def solution(mesh):
    in_specs = (P("blk", None), P(), P("blk", None))
    out_specs = P("blk", None)
    return jax.shard_map(
        per_device, mesh=mesh, in_specs=in_specs, out_specs=out_specs, check_vma=False
    )
```

```python
import math

import jax
import jax.numpy as jnp
from jax import lax
from jax.experimental import pallas as pl
from jax.experimental.pallas import tpu as pltpu
from jax.sharding import PartitionSpec as P

F32, BF16, F8 = jnp.float32, jnp.bfloat16, jnp.float8_e4m3fn
TILE_SCALE, VEC_SCALE = 2.0**16, 256.0
SUBLANES, LANES = 8, 128
WIDTH = 1536
VMEM_LIMIT = 36 * 2**20
MOST_FLOPS = 10**10
LANE_FLOPS = 10**10
SELF_FLOPS = 10**9
VISIT_FLOPS = 3 * 10**9
ROOT_LOG2E = math.sqrt(math.log2(math.e))


def dot(a, b, contract_b=0):
    dims = (((1,), (contract_b,)), ((), ()))
    return lax.dot_general(a, b, dims, preferred_element_type=F32)


def split(x):
    high = x.astype(BF16)
    return high, (x - high.astype(F32)).astype(BF16)


def split_points(points, gain):
    high, low = split(points * (gain * ROOT_LOG2E))
    whole = high.astype(F32) + low.astype(F32)
    return high, low, -0.5 * jnp.sum(whole * whole, axis=1, keepdims=True)


def row_factor(points, gain):
    high, low, half = split_points(points, gain)
    return jnp.concatenate([high, low, high, low], axis=1), half


def column_factor(points, gain):
    high, low, half = split_points(points, gain)
    half = jnp.broadcast_to(half, points.shape).T[:1, :]
    return jnp.concatenate([high, high, low, low], axis=1), half


def vector_parts(vec, axis, most=None):
    if most is None:
        most = jnp.max(jnp.abs(vec))
    most = jnp.maximum(most, 1e-30)
    coarse = (vec * (VEC_SCALE / most)).astype(F8)
    return jnp.concatenate(split(vec), axis=axis), coarse, most / (VEC_SCALE * TILE_SCALE)


def split_vectors(vec_t, most=None):
    return vector_parts(vec_t, 0, most)


def column_vectors(vec_t):
    return vector_parts(vec_t.T, 1)


def apply_strip(tile_high, tile_low, vec, rhs):
    both = dot(vec[0], tile_high)
    return both[:rhs] + both[rhs:] + dot(vec[1], tile_low) * vec[2]


def tile_strip(rows, column, at):
    cross = dot(rows[0], column[0][at, :], 1)
    tile = jnp.exp2(cross + rows[1] + column[1][:, at])
    high = tile.astype(BF16)
    return high, ((tile - high.astype(F32)) * TILE_SCALE).astype(F8)


def strips(points):
    return [slice(at, at + WIDTH) for at in range(0, points, WIDTH)]


def unpack_vectors(packed, rhs, points):
    rows = range(points, points + rhs * points // LANES, rhs)
    return jnp.concatenate([packed[at : at + rhs, :] for at in rows], axis=1)


def unpack_gain(packed):
    end = packed.shape[0] - SUBLANES
    return packed[end : end + 1, :]


def lane_kernel(out):
    out[...] = lax.broadcasted_iota(jnp.int32, out.shape, 1)


def self_kernel(lane, pts, vec_t, gain, out, packed, vec_out):
    rhs, points = vec_t.shape
    packed[:points, :] = pts[...]
    for at in range(points // LANES):
        rows = slice(points + at * rhs, points + (at + 1) * rhs)
        packed[rows, :] = vec_t[:, at * LANES : (at + 1) * LANES]
    end = points + rhs * points // LANES
    packed[end:, :] = jnp.broadcast_to(gain[...], (SUBLANES, LANES))
    vec_out[...] = vec_t[...]
    column = column_factor(pts[...], gain[...])
    rows = row_factor(pts[...], gain[...])
    vec = split_vectors(vec_t[...])
    for at in strips(points):
        high, low = tile_strip(rows, column, at)
        out[:, at] = apply_strip(high, low, vec, rhs)


def from_columns(high, low, vec, at, rhs):
    both = dot(high, vec[0][at, :])
    return both[:, :rhs] + both[:, rhs:] + dot(low, vec[1][at, :]) * vec[2]


def visit_kernel(other, own, back, tile_high, tile_low):
    rhs, points = back.shape
    gain = unpack_gain(own)
    vec = column_vectors(unpack_vectors(own, rhs, points))
    column = column_factor(own[:points, :], gain)
    rows = row_factor(other[...], gain)
    partial = None
    for at in strips(points):
        high, low = tile_strip(rows, column, at)
        tile_high[:, at] = high
        tile_low[:, at] = low
        added = from_columns(high, low, vec, at, rhs)
        partial = added if partial is None else partial + added
    back[...] = partial.T


def most_kernel(vec_t, after, out):
    out[...] = jnp.full(out.shape, jnp.max(jnp.abs(vec_t[...])), F32)


def mate_kernel(other, mate, partial, most, back, most_out):
    rhs, points = back.shape
    most_out[...] = most[...]
    gain = unpack_gain(mate)
    rows = row_factor(mate[:points, :], gain)
    vec = split_vectors(unpack_vectors(mate, rhs, points))
    column = column_factor(other[...], gain)
    for at in strips(points):
        high, low = tile_strip(rows, column, at)
        back[:, at] = partial[:, at] + apply_strip(high, low, vec, rhs)


def own_kernel(tile_high, tile_low, other_vec, most, own, mate, out):
    rhs, points = out.shape
    gain = unpack_gain(own)
    vec = split_vectors(other_vec[...], most[:1, :1])
    column = column_factor(own[:points, :], gain)
    rows = row_factor(mate[:points, :], gain)
    mate_vec = split_vectors(unpack_vectors(mate, rhs, points))
    for at in strips(points):
        gained = apply_strip(tile_high[:, at], tile_low[:, at], vec, rhs)
        high, low = tile_strip(rows, column, at)
        out[:, at] = gained + apply_strip(high, low, mate_vec, rhs)


def per_device(points, inv_scale, vectors):
    rows, features = points.shape
    rhs = vectors.shape[1]
    n = lax.axis_size("blk")
    ahead = [(i, (i - 2) % n if i % 2 == 0 else (i + 2) % n) for i in range(n)]
    back_home = [(d, s) for s, d in ahead]
    swap = [(i, i ^ 1) for i in range(n)]
    def call(kernel, outs, *args, flops):
        return pl.pallas_call(
            kernel,
            out_shape=outs,
            compiler_params=pltpu.CompilerParams(vmem_limit_bytes=VMEM_LIMIT),
            cost_estimate=pl.CostEstimate(
                flops=flops, bytes_accessed=rows, transcendentals=rows
            ),
        )(*args)

    gain = inv_scale[None, :]
    vec_t = vectors.T
    product = jax.ShapeDtypeStruct((rhs, rows), F32)
    tile, rest = [jax.ShapeDtypeStruct((rows, rows), kind) for kind in (BF16, F8)]
    packed = jax.ShapeDtypeStruct((rows + rhs * rows // LANES + SUBLANES, LANES), F32)

    visitor = lax.ppermute(points, "blk", ahead)
    lane_shape = jax.ShapeDtypeStruct((SUBLANES, LANES), jnp.int32)
    lane = call(lane_kernel, lane_shape, flops=LANE_FLOPS)
    total, own, vec_copy = call(
        self_kernel,
        (product, packed, product),
        *(lane, points, vec_t, gain),
        flops=SELF_FLOPS,
    )
    mate = lax.ppermute(own, "blk", swap)
    visitor_vec = lax.ppermute(vec_copy, "blk", ahead)
    partial, high, low = call(
        visit_kernel, (product, tile, rest), visitor, own, flops=VISIT_FLOPS
    )
    most_shape = jax.ShapeDtypeStruct((SUBLANES, LANES), F32)
    most = call(most_kernel, most_shape, visitor_vec, partial, flops=MOST_FLOPS)
    partial, most = call(
        mate_kernel, (product, most_shape), visitor, mate, partial, most, flops=SELF_FLOPS
    )
    returned = lax.ppermute(partial, "blk", back_home)
    gained = call(
        own_kernel, product, *(high, low, visitor_vec, most, own, mate), flops=SELF_FLOPS
    )
    return (total + gained + returned).T


def solution(mesh):
    in_specs = (P("blk", None), P(), P("blk", None))
    out_specs = P("blk", None)
    return jax.shard_map(
        per_device, mesh=mesh, in_specs=in_specs, out_specs=out_specs, check_vma=False
    )
```
